32 devices in a mesh: pole: 2 (over y), row: 4 (over z), col: 4 (over x, core).
Axes of the slice: x: 2, y: 2, z: 4, core: 2. Of those that a mesh axis runs over, the one named last changes fastest.
Arguments:
- inverse_blocks: bfloat16 [128, 64, 128, 128], P(('pole', 'row'), 'col'), parts along dimension 0, may hold values from -6 to 6
- panel: bfloat16 [8, 32, 128, 128], P(('pole', 'row')), parts along dimension 0, may hold values from -0.09375 to 0.09375
- lists: int32 [4, 32], replicated, may hold values from 0 to 63, as said below
- diag_inverse: float32 [8, 128, 128], P(('pole', 'col')), parts along dimension 0, may hold values from -6 to 6
Outputs:
- offdiag: bfloat16 [8, 64, 128, 128], P(('pole', 'col'), 'row'), parts along dimension 0
- diagonal: float32 [8, 128, 128], P(('pole', 'col')), parts along dimension 0
The draws below stay inside these ranges and needn't reach their ends.
There are 2 independent parts, one for each index of `pole`. The reference program is written for one: setup_inputs(seed, part) draws one part's arguments, and reference() takes and returns one part's arrays. A program takes and returns all parts, laid end to end along the dimension named above; an argument that names none is the same for every part. Nothing has to cross between parts.
Inputs may be any that keep to these rules, and one draw needn't show every extreme that they name: `lists`: each row holds 32 different ancestor block numbers in increasing order; at most 6 of them lie in any aligned group of 8 consecutive numbers, and every row has exactly 6 in some group.
All inputs are finite; a program needn't handle non-finite values.
Results may differ from the reference program's by a relative error of at most 0.0075.
Values may be sent and summed in bfloat16 or wider, within the bound.
A program may use at most 128 MiB of HBM per device.

```python
import jax
import jax.numpy as jnp
from jax import lax

S = 128
NB = 64
NL = 32
GROUP = 8
NK = 4


def draw_lists(key, part):
    key = jax.random.fold_in(key, 7)
    first, second = jax.random.split(key)
    group_count = NB // GROUP
    pattern = jnp.array([6, 6, 5, 4, 4, 3, 2, 2], jnp.int32)
    counts = jax.vmap(lambda sub: jax.random.permutation(sub, pattern))(jax.random.split(first, NK))
    scores = jax.random.randint(second, (NK, group_count, GROUP), 0, 1 << 20) * GROUP + jnp.arange(GROUP, dtype=jnp.int32)
    order = jnp.argsort(scores, axis=2)
    ranks = jnp.argsort(order, axis=2)
    chosen = (ranks < counts[:, :, None]).reshape(NK, NB)
    numbers = jnp.arange(NB, dtype=jnp.int32)[None, :]
    keys = jnp.where(chosen, numbers, NB + numbers)
    return jnp.sort(keys, axis=1)[:, :NL].astype(jnp.int32)


def block_levels(stream_key, extent, shards, low, top_value):
    factor_of = 1.0
    for axis_at, shards_of in shards:
        steps = jax.random.uniform(jax.random.fold_in(jax.random.fold_in(stream_key, 6), axis_at), (shards_of,), jnp.float32, low / len(shards), top_value / len(shards))
        factor_of = factor_of * jnp.repeat(jnp.exp(steps), extent[axis_at] // shards_of).reshape((-1,) + (1,) * (len(extent) - 1 - axis_at))
    return factor_of


def bell_draw(own_key, shape, deviation, reach, cuts=(), kind=jnp.bfloat16):
    loudness = block_levels(own_key, shape, cuts, -0.22, 0.18) if cuts else 1.0
    values = jax.random.normal(own_key, shape, jnp.float32) * deviation * loudness
    return jnp.minimum(jnp.maximum(values, -reach), reach).astype(kind)


def setup_inputs(seed: int = 0, part: int = 0) -> dict:
    key_of = jax.random.split(jax.random.key(seed), 5)
    part_splits = jax.random.split(jax.random.fold_in(key_of[4], part), 5)
    inverse_blocks = bell_draw(part_splits[0], (NB, NB, S, S), 1.0, 6.0, ((0, 4), (1, 4)))
    panel = bell_draw(part_splits[1], (NK, NL, S, S), (NL * S) ** -0.5, 0.09375, ((0, 4),))
    lists = draw_lists(jax.random.fold_in(key_of[4], 71), part)
    diag_inverse = bell_draw(part_splits[3], (NK, S, S), 1.0, 6.0, ((0, 4),), jnp.float32)
    return {"inverse_blocks": inverse_blocks, "panel": panel, "lists": lists, "diag_inverse": diag_inverse}


def reference(inverse_blocks, panel, lists, diag_inverse):
    total = inverse_blocks.shape[0]
    width = inverse_blocks.shape[2]
    matrix = inverse_blocks.transpose(0, 2, 1, 3).reshape(total * width, total * width)
    numbers = jnp.arange(total, dtype=jnp.int32)

    def one_super(inputs):
        rows, blocks = inputs
        onehot = (rows[:, None] == numbers[None, :]).astype(jnp.float32)
        spread = jnp.einsum("ln,lab->nab", onehot, blocks.astype(jnp.float32), precision=lax.Precision.HIGHEST)
        flat_exact = spread.reshape(total * width, width)
        flat_low = flat_exact.astype(jnp.bfloat16)
        product = jnp.dot(matrix, flat_low, preferred_element_type=jnp.float32)
        quad = jnp.dot(flat_exact.T, product, precision=lax.Precision.HIGHEST)
        keep = jnp.sum(onehot, axis=0)
        below = (-product.reshape(total, width, width) * keep[:, None, None]).astype(jnp.bfloat16)
        return below, quad

    offdiag, quad = lax.map(one_super, (lists, panel))
    diagonal = diag_inverse + quad
    return offdiag, diagonal
```

```python
import functools

import jax
import jax.numpy as jnp
from jax import lax
from jax.experimental import pallas as pl
from jax.experimental.pallas import tpu as pltpu
from jax.sharding import PartitionSpec as P

GROUP = 8
MOST = 6
MESH = pl.DeviceIdType.MESH


def slot_count(width, n_list):
    if width % GROUP == 0:
        count = width // GROUP * MOST
    elif GROUP % width == 0:
        count = min(width, MOST)
    else:
        count = width
    return min(count, n_list)


def kernel(
    n_row, n_col, k_col, rows_here, cols_here, n_list, slots_r, slots_c,
    lists, inv_hbm, panel_hbm, dinv, off, diag,
    inv, panel, got, cur, xs, part, acc, stage, x_stage, sib_in, dest_sib, dest_x,
    quadx, tot, quad_in,
    load_sem, up_s, down_s, x_r, qx_s, qx_r, st_s, sib_r, dsib_r, xs_s, dx_r, q_s, q_r,
):
    r = lax.axis_index("row")
    c = lax.axis_index("col")
    width = inv.shape[-1]
    chip, core = c // 2, c % 2
    sibling = chip * 2 + 1 - core
    half = slots_r // 2
    n_chip = n_col // 2
    row_base, col_base = r * rows_here, c * cols_here
    c_src = row_base // cols_here

    load_panel = pltpu.make_async_copy(panel_hbm.at[0], panel, load_sem.at[0])
    load_inv = pltpu.make_async_copy(inv_hbm, inv, load_sem.at[1])
    load_panel.start()
    load_inv.start()

    barrier = pltpu.get_barrier_semaphore()
    for step in range(1, n_row):
        pl.semaphore_signal(barrier, inc=1, device_id={"row": lax.rem(r + step, n_row)}, device_id_type=MESH)
    for step in range(1, n_col):
        pl.semaphore_signal(barrier, inc=1, device_id={"col": lax.rem(c + step, n_col)}, device_id_type=MESH)

    def before(k, bound):
        total = jnp.int32(0)
        for l in range(n_list):
            total += jnp.where(lists[k, l] < bound, 1, 0).astype(jnp.int32)
        return total

    def first(begin, slots):
        return jnp.minimum(begin, n_list - slots)

    cur[slots_c] = jnp.zeros((width, width), cur.dtype)
    tot[slots_r] = jnp.zeros((width, width), tot.dtype)
    mine = first(before(r, col_base), slots_c)
    load_panel.wait()
    got[r] = panel[pl.ds(mine, slots_c)]
    pl.semaphore_wait(barrier, n_row + n_col - 2)

    def go_up(k):
        return pltpu.make_async_remote_copy(
            got.at[k], got.at[k], up_s.at[k], x_r.at[k], device_id={"row": r + 1}, device_id_type=MESH)

    def go_down(k):
        return pltpu.make_async_remote_copy(
            got.at[k], got.at[k], down_s.at[k], x_r.at[k], device_id={"row": r - 1}, device_id_type=MESH)

    def send_rows(k):
        return pltpu.make_async_remote_copy(
            got.at[k], quadx.at[k % k_col], qx_s.at[k], qx_r.at[k % k_col],
            device_id={"col": k // k_col}, device_id_type=MESH)

    def send_to_owner(k, h):
        return pltpu.make_async_remote_copy(
            stage.at[k, h], dest_sib.at[k % k_col, h], st_s.at[k, h], dsib_r.at[k % k_col, h],
            device_id={"col": k // k_col}, device_id_type=MESH)

    def send_to_sibling(k, h):
        return pltpu.make_async_remote_copy(
            stage.at[k, h], sib_in.at[k], st_s.at[k, h], sib_r.at[k],
            device_id={"col": sibling}, device_id_type=MESH)

    def send_across(k):
        return pltpu.make_async_remote_copy(
            x_stage.at[k], dest_x.at[k % k_col, chip, core], xs_s.at[k],
            dx_r.at[k % k_col, chip, core],
            device_id={"col": k // k_col}, device_id_type=MESH)

    def use(k):
        owner = k // k_col
        at = k % k_col

        @pl.when(k != r)
        def _():
            go_up(k).wait_recv()

        @pl.when((k <= r) & (r < n_row - 1))
        def _():
            go_up(k).start()

        @pl.when((k >= r) & (r > 0))
        def _():
            go_down(k).start()

        @pl.when((c == c_src) & (owner == c))
        def _():
            quadx[at] = got[k]

        @pl.when((c == c_src) & (owner != c))
        def _():
            send_rows(k).start()

        begin = before(k, col_base)
        base = first(begin, slots_c)
        cur[0:slots_c] = got[k]
        p = begin
        for j in range(cols_here):
            hit = lists[k, jnp.minimum(p, n_list - 1)] == col_base + j
            slot = jnp.where(hit, jnp.clip(p - base, 0, slots_c - 1), slots_c)
            xs[j * width : (j + 1) * width, :] = cur[slot]
            p += hit.astype(jnp.int32)

        @pl.when(k == r)
        def _():
            load_inv.wait()

        row_first = first(before(k, row_base), slots_r)

        def half_step(turn, carry):
            h = (core + 1 + turn) % 2
            lines = []
            for s in range(half):
                i = jnp.clip(lists[k, row_first + h * half + s] - row_base, 0, rows_here - 1)
                blocks = inv[i]
                lines.append(jnp.concatenate([blocks[j] for j in range(cols_here)], axis=1))
            left = jnp.concatenate(lines, axis=0)
            part[...] = jnp.dot(left, xs[...], preferred_element_type=jnp.float32)

            @pl.when(owner == c)
            def _():
                acc[at, h] = part[...]

            @pl.when(owner == sibling)
            def _():
                stage[k, h] = part[...].astype(stage.dtype)
                send_to_owner(k, h).start()

            @pl.when((owner // 2 != chip) & (turn == 0))
            def _():
                stage[k, h] = part[...].astype(stage.dtype)
                send_to_sibling(k, h).start()

            @pl.when((owner // 2 != chip) & (turn == 1))
            def _():
                send_to_sibling(k, h).wait_recv()
                x_stage[k] = (part[...] + sib_in[k].astype(jnp.float32)).astype(x_stage.dtype)
                send_across(k).start()

            return carry

        lax.fori_loop(0, 2, half_step, 0)

    def turn_step(t, carry):
        s = (t + 1) // 2
        k = r + jnp.where(t % 2 == 1, -s, s)

        @pl.when((k >= 0) & (k < n_row))
        def _():
            use(k)

        return carry

    lax.fori_loop(0, 2 * n_row - 1, turn_step, 0)

    def finish(at, carry):
        k = c * k_col + at

        @pl.when(c != c_src)
        def _():
            send_rows(k).wait_recv()

        for h in range(2):
            send_to_owner(k, h).wait_recv()
        total = acc[at].astype(jnp.float32) + dest_sib[at].astype(jnp.float32)
        tot[0:slots_r] = total.reshape(slots_r, width, width)
        for step in range(1, n_chip):
            other = lax.rem(chip + step, n_chip)
            for h in range(2):
                pltpu.make_async_remote_copy(
                    x_stage.at[k], dest_x.at[at, other, h], xs_s.at[k], dx_r.at[at, other, h],
                    device_id={"col": other * 2 + h}, device_id_type=MESH).wait_recv()
            come = dest_x[at, other].astype(jnp.float32)
            tot[0:slots_r] = tot[0:slots_r] + come.reshape(slots_r, width, width)

        begin = before(k, row_base)
        row_first = first(begin, slots_r)
        p = begin
        for i in range(rows_here):
            hit = lists[k, jnp.minimum(p, n_list - 1)] == row_base + i
            slot = jnp.where(hit, jnp.clip(p - row_first, 0, slots_r - 1), slots_r)
            off[at, i] = (-tot[slot]).astype(off.dtype)
            p += hit.astype(jnp.int32)

        col_first = first(before(k, c_src * cols_here), slots_c)
        cur[0:slots_c] = quadx[at]
        lines = []
        for s in range(slots_r):
            position = row_first + s
            number = lists[k, position] - row_base
            valid = (number >= 0) & (number < rows_here)
            slot = jnp.where(valid, jnp.clip(position - col_first, 0, slots_c - 1), slots_c)
            lines.append(cur[slot])
        left = jnp.concatenate(lines, axis=0)
        right = tot[0:slots_r].reshape(slots_r * width, width)
        high = right.astype(jnp.bfloat16)
        low = (right - high.astype(jnp.float32)).astype(jnp.bfloat16)
        both = lax.dot_general(
            left, jnp.concatenate([high, low], axis=1), (((0,), (0,)), ((), ())),
            preferred_element_type=jnp.float32)
        quad_in[r, at] = (both[:, :width] + both[:, width:]).astype(quad_in.dtype)
        return carry

    lax.fori_loop(0, k_col, finish, 0)

    def share(other):
        return pltpu.make_async_remote_copy(
            quad_in.at[r], quad_in.at[r], q_s.at[other], q_r.at[r],
            device_id={"row": other}, device_id_type=MESH)

    def take(other):
        return pltpu.make_async_remote_copy(
            quad_in.at[other], quad_in.at[other], q_s.at[other], q_r.at[other],
            device_id={"row": other}, device_id_type=MESH)

    def start_share(step, carry):
        share(lax.rem(r + step, n_row)).start()
        return carry

    lax.fori_loop(1, n_row, start_share, 0)

    def drain(k, carry):
        owner = k // k_col

        @pl.when((k <= r) & (r < n_row - 1))
        def _():
            go_up(k).wait_send()

        @pl.when((k >= r) & (r > 0))
        def _():
            go_down(k).wait_send()

        @pl.when((c == c_src) & (owner != c))
        def _():
            send_rows(k).wait_send()

        @pl.when(owner == sibling)
        def _():
            send_to_owner(k, 0).wait_send()
            send_to_owner(k, 1).wait_send()

        @pl.when(owner // 2 != chip)
        def _():
            send_to_sibling(k, 1 - core).wait_send()
            send_across(k).wait_send()

        return carry

    lax.fori_loop(0, n_row, drain, 0)

    def wait_share(step, carry):
        other = lax.rem(r + step, n_row)
        take(other).wait_recv()
        share(other).wait_send()
        return carry

    lax.fori_loop(1, n_row, wait_share, 0)

    quad = quad_in[0].astype(jnp.float32)
    for other in range(1, n_row):
        quad = quad + quad_in[other].astype(jnp.float32)
    diag[...] = dinv[...] + quad


def per_device(n_row, n_col, inverse_blocks, panel, lists, diag_inverse):
    rows_here, cols_here, width, _ = inverse_blocks.shape
    n_list = panel.shape[1]
    k_col = diag_inverse.shape[0]
    slots_r = slot_count(rows_here, n_list)
    slots_c = slot_count(cols_here, n_list)
    half = slots_r // 2
    n_super = n_row
    low, full = inverse_blocks.dtype, jnp.float32
    part = (half * width, width)
    dma = pltpu.SemaphoreType.DMA
    vmem = pl.BlockSpec(memory_space=pltpu.VMEM)
    return pl.pallas_call(
        functools.partial(
            kernel, n_row, n_col, k_col, rows_here, cols_here, n_list, slots_r, slots_c),
        out_shape=(
            jax.ShapeDtypeStruct((k_col, rows_here, width, width), low),
            jax.ShapeDtypeStruct((k_col, width, width), full),
        ),
        in_specs=[
            pl.BlockSpec(memory_space=pltpu.SMEM),
            pl.BlockSpec(memory_space=pl.ANY),
            pl.BlockSpec(memory_space=pl.ANY),
            vmem,
        ],
        out_specs=(vmem, vmem),
        scratch_shapes=[
            pltpu.VMEM(inverse_blocks.shape, low),
            pltpu.VMEM(panel.shape[1:], low),
            pltpu.VMEM((n_super, slots_c, width, width), low),
            pltpu.VMEM((slots_c + 1, width, width), low),
            pltpu.VMEM((cols_here * width, width), low),
            pltpu.VMEM(part, full),
            pltpu.VMEM((k_col, 2) + part, full),
            pltpu.VMEM((n_super, 2) + part, low),
            pltpu.VMEM((n_super,) + part, low),
            pltpu.VMEM((n_super,) + part, low),
            pltpu.VMEM((k_col, 2) + part, low),
            pltpu.VMEM((k_col, n_col // 2, 2) + part, low),
            pltpu.VMEM((k_col, slots_c, width, width), low),
            pltpu.VMEM((slots_r + 1, width, width), full),
            pltpu.VMEM((n_row, k_col, width, width), low),
            dma((2,)),
            dma((n_super,)),
            dma((n_super,)),
            dma((n_super,)),
            dma((n_super,)),
            dma((k_col,)),
            dma((n_super, 2)),
            dma((n_super,)),
            dma((k_col, 2)),
            dma((n_super,)),
            dma((k_col, n_col // 2, 2)),
            dma((n_row,)),
            dma((n_row,)),
        ],
        compiler_params=pltpu.CompilerParams(
            collective_id=0, has_side_effects=True, vmem_limit_bytes=50 * 1024 * 1024),
        name="selected_inverse",
    )(lists, inverse_blocks, panel, diag_inverse)


def solution(mesh):
    in_specs = (
        P(("pole", "row"), "col", None, None),
        P(("pole", "row"), None, None, None),
        P(),
        P(("pole", "col"), None, None),
    )
    out_specs = (P(("pole", "col"), "row", None, None), P(("pole", "col"), None, None))
    return jax.shard_map(
        functools.partial(per_device, mesh.shape["row"], mesh.shape["col"]),
        mesh=mesh, in_specs=in_specs, out_specs=out_specs, check_vma=False)
```

```python
import functools

import jax
import jax.numpy as jnp
from jax import lax
from jax.experimental import pallas as pl
from jax.experimental.pallas import tpu as pltpu
from jax.sharding import PartitionSpec as P

GROUP = 8
MOST = 6
CHUNKS = 2
MESH = pl.DeviceIdType.MESH


def slot_count(width, n_list):
    if width % GROUP == 0:
        count = width // GROUP * MOST
    elif GROUP % width == 0:
        count = min(width, MOST)
    else:
        count = width
    return min(count, n_list)


def kernel(
    n_row, n_col, k_col, rows_here, cols_here, n_list, slots_r, slots_c,
    lists, inv_hbm, panel_hbm, dinv, off, diag,
    inv, panel, got, cur, xs, part, acc, stage, x_stage, sib_in, dest_x,
    quadx, tot, quad_out, quad_in,
    load_sem, up_s, down_s, x_r, qx_s, qx_r, st_s, sib_r, xs_s, dx_r, q_s, q_r,
):
    r = lax.axis_index("row")
    c = lax.axis_index("col")
    width = inv.shape[-1]
    chip, core = c // 2, c % 2
    sibling = chip * 2 + 1 - core
    half = slots_r // 2
    n_chip = n_col // 2
    row_base, col_base = r * rows_here, c * cols_here
    c_src = row_base // cols_here

    load_panel = pltpu.make_async_copy(panel_hbm.at[0], panel, load_sem.at[0])
    load_inv = pltpu.make_async_copy(inv_hbm, inv, load_sem.at[1])
    load_panel.start()
    load_inv.start()

    barrier = pltpu.get_barrier_semaphore()
    def greet(at, carry):
        @pl.when((at // n_col != r) | (at % n_col != c))
        def _():
            pl.semaphore_signal(
                barrier, inc=1, device_id={"row": at // n_col, "col": at % n_col}, device_id_type=MESH)

        return carry

    lax.fori_loop(0, n_row * n_col, greet, 0)

    def before(k, bound):
        total = jnp.int32(0)
        for l in range(n_list):
            total += jnp.where(lists[k, l] < bound, 1, 0).astype(jnp.int32)
        return total

    def first(begin, slots):
        return jnp.minimum(begin, n_list - slots)

    cur[slots_c] = jnp.zeros((width, width), cur.dtype)
    tot[slots_r] = jnp.zeros((width, width), tot.dtype)
    mine = first(before(r, col_base), slots_c)
    load_panel.wait()
    got[r] = panel[pl.ds(mine, slots_c)]
    pl.semaphore_wait(barrier, n_row * n_col - 1)

    chunk = slots_c // CHUNKS

    def go(k, q, step, sems):
        piece = got.at[k, pl.ds(q * chunk, chunk)]
        return pltpu.make_async_remote_copy(
            piece, piece, sems.at[k, q], x_r.at[k, q],
            device_id={"row": r + step}, device_id_type=MESH)

    def go_up(k, q):
        return go(k, q, 1, up_s)

    def go_down(k, q):
        return go(k, q, -1, down_s)

    def send_rows(k):
        return pltpu.make_async_remote_copy(
            got.at[k], quadx.at[k % k_col], qx_s.at[k], qx_r.at[k % k_col],
            device_id={"col": k // k_col}, device_id_type=MESH)

    def send_to_sibling(k, h):
        return pltpu.make_async_remote_copy(
            stage.at[k], sib_in.at[k], st_s.at[k], sib_r.at[k],
            device_id={"col": sibling}, device_id_type=MESH)

    def send_sum(k, target, which):
        return pltpu.make_async_remote_copy(
            x_stage.at[k], dest_x.at[k, chip, core], xs_s.at[k, which], dx_r.at[k, chip, core],
            device_id={"col": target}, device_id_type=MESH)

    def take_sum(k, q, h):
        return pltpu.make_async_remote_copy(
            x_stage.at[k], dest_x.at[k, q, h], xs_s.at[k, 0], dx_r.at[k, q, h],
            device_id={"col": q * 2 + h}, device_id_type=MESH)

    def share(k, target):
        return pltpu.make_async_remote_copy(
            quad_out.at[k], quad_in.at[r, k % k_col], q_s.at[k, target], q_r.at[r, k % k_col],
            device_id={"row": target, "col": k // k_col}, device_id_type=MESH)

    def take_share(at, other):
        return pltpu.make_async_remote_copy(
            quad_out.at[0], quad_in.at[other, at], q_s.at[0, 0], q_r.at[other, at],
            device_id={"row": other}, device_id_type=MESH)

    def crosses(k):
        return (k // k_col) // 2 != c_src // 2

    def lends_rows(k):
        return (c == c_src) & (k // k_col == sibling)

    def has_quad(k):
        return (crosses(k) & (c == c_src)) | (jnp.logical_not(crosses(k)) & (k // k_col == c))

    def pass_on(k, q):
        @pl.when(k != r)
        def _():
            go_up(k, q).wait_recv()

        @pl.when((k <= r) & (r < n_row - 1))
        def _():
            go_up(k, q).start()

        @pl.when((k >= r) & (r > 0))
        def _():
            go_down(k, q).start()

    def use(k):
        owner = k // k_col

        @pl.when(lends_rows(k))
        def _():
            send_rows(k).start()

        begin = before(k, col_base)
        base = first(begin, slots_c)
        cur[0:slots_c] = got[k]
        p = begin
        for j in range(cols_here):
            hit = lists[k, jnp.minimum(p, n_list - 1)] == col_base + j
            slot = jnp.where(hit, jnp.clip(p - base, 0, slots_c - 1), slots_c)
            xs[j * width : (j + 1) * width, :] = cur[slot]
            p += hit.astype(jnp.int32)

        @pl.when(k == r)
        def _():
            load_inv.wait()

        row_first = first(before(k, row_base), slots_r)

        def half_step(turn, carry):
            h = (core + 1 + turn) % 2
            lines = []
            for s in range(half):
                i = jnp.clip(lists[k, row_first + h * half + s] - row_base, 0, rows_here - 1)
                blocks = inv[i]
                lines.append(jnp.concatenate([blocks[j] for j in range(cols_here)], axis=1))
            left = jnp.concatenate(lines, axis=0)
            part[...] = jnp.dot(left, xs[...], preferred_element_type=jnp.float32)

            @pl.when(turn == 0)
            def _():
                stage[k] = part[...].astype(stage.dtype)
                send_to_sibling(k, h).start()

            @pl.when(turn == 1)
            def _():
                send_to_sibling(k, h).wait_recv()
                acc[k] = part[...] + sib_in[k].astype(jnp.float32)
                x_stage[k] = acc[k].astype(x_stage.dtype)

                @pl.when(owner != c)
                def _():
                    send_sum(k, owner, 0).start()

                @pl.when(crosses(k) & (c != c_src))
                def _():
                    send_sum(k, c_src, 1).start()

            return carry

        lax.fori_loop(0, 2, half_step, 0)

    def finish(k):
        owner = k // k_col
        at = k % k_col

        def gather_half(h, carry):
            def from_chip(q, carry):
                @pl.when((q != chip) | (h != core))
                def _():
                    take_sum(k, q, h).wait_recv()
                    come = dest_x[k, q, h].astype(jnp.float32).reshape(half, width, width)
                    where = pl.ds(h * half, half)

                    @pl.when(q == 0)
                    def _():
                        tot[where] = come

                    @pl.when(q > 0)
                    def _():
                        tot[where] = tot[where] + come

                @pl.when((q == chip) & (h == core))
                def _():
                    come = acc[k].reshape(half, width, width)
                    where = pl.ds(h * half, half)

                    @pl.when(q == 0)
                    def _():
                        tot[where] = come

                    @pl.when(q > 0)
                    def _():
                        tot[where] = tot[where] + come

                return carry

            return lax.fori_loop(0, n_chip, from_chip, carry)

        lax.fori_loop(0, 2, gather_half, 0)
        begin = before(k, row_base)
        row_first = first(begin, slots_r)

        @pl.when(has_quad(k))
        def _():
            col_first = first(before(k, c_src * cols_here), slots_c)

            @pl.when(c == c_src)
            def _():
                cur[0:slots_c] = got[k]

            @pl.when(c != c_src)
            def _():
                send_rows(k).wait_recv()
                cur[0:slots_c] = quadx[at]

            lines = []
            for s in range(slots_r):
                position = row_first + s
                number = lists[k, position] - row_base
                valid = (number >= 0) & (number < rows_here)
                slot = jnp.where(valid, jnp.clip(position - col_first, 0, slots_c - 1), slots_c)
                lines.append(cur[slot])
            left = jnp.concatenate(lines, axis=0)
            right = tot[0:slots_r].reshape(slots_r * width, width)
            high = right.astype(jnp.bfloat16)
            low = (right - high.astype(jnp.float32)).astype(jnp.bfloat16)
            both = lax.dot_general(
                left, jnp.concatenate([high, low], axis=1), (((0,), (0,)), ((), ())),
                preferred_element_type=jnp.float32)
            quad_out[k] = (both[:, :width] + both[:, width:]).astype(quad_out.dtype)

            def start_share(other, carry):
                @pl.when((other != r) | (owner != c))
                def _():
                    share(k, other).start()

                return carry

            lax.fori_loop(0, n_row, start_share, 0)

            @pl.when(owner == c)
            def _():
                quad_in[r, at] = quad_out[k]

        @pl.when(owner == c)
        def _():
            p = begin
            for i in range(rows_here):
                hit = lists[k, jnp.minimum(p, n_list - 1)] == row_base + i
                slot = jnp.where(hit, jnp.clip(p - row_first, 0, slots_r - 1), slots_r)
                off[at, i] = (-tot[slot]).astype(off.dtype)
                p += hit.astype(jnp.int32)

    def inside(k):
        return (k >= 0) & (k < n_row)

    def step(s, carry):
        def each(lap, body):
            k = r + jnp.where(lap == 0, -s, s)

            @pl.when(inside(k) & ((s > 0) | (lap == 0)))
            def _():
                body(k)

        def pass_step(i, carry):
            each(i % 2, lambda k: pass_on(k, i // 2))
            return carry

        lax.fori_loop(0, 2 * CHUNKS, pass_step, 0)

        def use_step(lap, carry):
            each(lap, use)
            return carry

        lax.fori_loop(0, 2, use_step, 0)

        def finish_step(lap, carry):
            last = s - 1
            k = r + jnp.where(lap == 0, -last, last)

            @pl.when(inside(k) & ((last > 0) | ((last == 0) & (lap == 0))))
            def _():
                owner = k // k_col

                @pl.when((owner == c) | (crosses(k) & (c == c_src)))
                def _():
                    finish(k)

            return carry

        lax.fori_loop(0, 2, finish_step, 0)
        return carry

    lax.fori_loop(0, n_row + 1, step, 0)

    def drain(k, carry):
        owner = k // k_col
        for q in range(CHUNKS):
            @pl.when((k <= r) & (r < n_row - 1))
            def _():
                go_up(k, q).wait_send()

            @pl.when((k >= r) & (r > 0))
            def _():
                go_down(k, q).wait_send()

        @pl.when(lends_rows(k))
        def _():
            send_rows(k).wait_send()

        send_to_sibling(k, 0).wait_send()

        @pl.when(owner != c)
        def _():
            send_sum(k, owner, 0).wait_send()

        @pl.when(crosses(k) & (c != c_src))
        def _():
            send_sum(k, c_src, 1).wait_send()

        @pl.when(has_quad(k))
        def _():
            def wait_share(other, carry):
                @pl.when((other != r) | (owner != c))
                def _():
                    share(k, other).wait_send()

                return carry

            lax.fori_loop(0, n_row, wait_share, 0)

        return carry

    lax.fori_loop(0, n_row, drain, 0)

    def arrive(at, carry):
        def one(other, carry):
            k = c * k_col + at

            @pl.when((other != r) | crosses(k))
            def _():
                take_share(at, other).wait_recv()

            return carry

        return lax.fori_loop(0, n_row, one, carry)

    lax.fori_loop(0, k_col, arrive, 0)

    quad = quad_in[0].astype(jnp.float32)
    for other in range(1, n_row):
        quad = quad + quad_in[other].astype(jnp.float32)
    diag[...] = dinv[...] + quad


def per_device(n_row, n_col, inverse_blocks, panel, lists, diag_inverse):
    rows_here, cols_here, width, _ = inverse_blocks.shape
    n_list = panel.shape[1]
    k_col = diag_inverse.shape[0]
    slots_r = slot_count(rows_here, n_list)
    slots_c = slot_count(cols_here, n_list)
    half = slots_r // 2
    n_super = n_row
    low, full = inverse_blocks.dtype, jnp.float32
    part = (half * width, width)
    dma = pltpu.SemaphoreType.DMA
    vmem = pl.BlockSpec(memory_space=pltpu.VMEM)
    return pl.pallas_call(
        functools.partial(
            kernel, n_row, n_col, k_col, rows_here, cols_here, n_list, slots_r, slots_c),
        out_shape=(
            jax.ShapeDtypeStruct((k_col, rows_here, width, width), low),
            jax.ShapeDtypeStruct((k_col, width, width), full),
        ),
        in_specs=[
            pl.BlockSpec(memory_space=pltpu.SMEM),
            pl.BlockSpec(memory_space=pl.ANY),
            pl.BlockSpec(memory_space=pl.ANY),
            vmem,
        ],
        out_specs=(vmem, vmem),
        scratch_shapes=[
            pltpu.VMEM(inverse_blocks.shape, low),
            pltpu.VMEM(panel.shape[1:], low),
            pltpu.VMEM((n_super, slots_c, width, width), low),
            pltpu.VMEM((slots_c + 1, width, width), low),
            pltpu.VMEM((cols_here * width, width), low),
            pltpu.VMEM(part, full),
            pltpu.VMEM((n_super,) + part, full),
            pltpu.VMEM((n_super,) + part, low),
            pltpu.VMEM((n_super,) + part, low),
            pltpu.VMEM((n_super,) + part, low),
            pltpu.VMEM((n_super, n_col // 2, 2) + part, low),
            pltpu.VMEM((k_col, slots_c, width, width), low),
            pltpu.VMEM((slots_r + 1, width, width), full),
            pltpu.VMEM((n_super, width, width), low),
            pltpu.VMEM((n_row, k_col, width, width), low),
            dma((2,)),
            dma((n_super, CHUNKS)),
            dma((n_super, CHUNKS)),
            dma((n_super, CHUNKS)),
            dma((n_super,)),
            dma((k_col,)),
            dma((n_super,)),
            dma((n_super,)),
            dma((n_super, 2)),
            dma((n_super, n_col // 2, 2)),
            dma((n_super, n_row)),
            dma((n_row, k_col)),
        ],
        compiler_params=pltpu.CompilerParams(
            collective_id=0, has_side_effects=True, vmem_limit_bytes=60 * 1024 * 1024),
        name="selected_inverse",
    )(lists, inverse_blocks, panel, diag_inverse)


def solution(mesh):
    in_specs = (
        P(("pole", "row"), "col", None, None),
        P(("pole", "row"), None, None, None),
        P(),
        P(("pole", "col"), None, None),
    )
    out_specs = (P(("pole", "col"), "row", None, None), P(("pole", "col"), None, None))
    return jax.shard_map(
        functools.partial(per_device, mesh.shape["row"], mesh.shape["col"]),
        mesh=mesh, in_specs=in_specs, out_specs=out_specs, check_vma=False)
```

```python
import functools

import jax
import jax.numpy as jnp
from jax import lax
from jax.experimental import pallas as pl
from jax.experimental.pallas import tpu as pltpu
from jax.sharding import PartitionSpec as P

GROUP = 8
MOST = 6
CHUNKS = 2
MESH = pl.DeviceIdType.MESH


def slot_count(width, n_list):
    if width % GROUP == 0:
        count = width // GROUP * MOST
    elif GROUP % width == 0:
        count = min(width, MOST)
    else:
        count = width
    return min(count, n_list)


def kernel(
    n_row, n_col, k_col, rows_here, cols_here, n_list, slots_r, slots_c,
    lists_hbm, inv_hbm, panel_hbm, off, diag,
    lists, inv, panel, got, cur, xs, part, acc, stage, x_stage, sib_in, dest_x,
    quadx, tot, quad_out, quad_in,
    load_sem, up_s, down_s, x_r, qx_s, qx_r, st_s, sib_r, xs_s, dx_r, q_s, q_r,
):
    r = lax.axis_index("row")
    c = lax.axis_index("col")
    width = inv.shape[-1]
    chip, core = c // 2, c % 2
    sibling = chip * 2 + 1 - core
    half = slots_r // 2
    n_chip = n_col // 2
    row_base, col_base = r * rows_here, c * cols_here
    c_src = row_base // cols_here

    load_panel = pltpu.make_async_copy(panel_hbm.at[0], panel, load_sem.at[0])
    load_inv = pltpu.make_async_copy(inv_hbm, inv, load_sem.at[1])
    load_lists = pltpu.make_async_copy(lists_hbm, lists, load_sem.at[2])
    load_lists.start()
    load_panel.start()

    barrier = pltpu.get_barrier_semaphore()
    def greet(at, carry):
        @pl.when((at // n_col != r) | (at % n_col != c))
        def _():
            pl.semaphore_signal(
                barrier, inc=1, device_id={"row": at // n_col, "col": at % n_col}, device_id_type=MESH)

        return carry

    lax.fori_loop(0, n_row * n_col, greet, 0)

    def before(k, bound):
        total = jnp.int32(0)
        for l in range(n_list):
            total += jnp.where(lists[k, l] < bound, 1, 0).astype(jnp.int32)
        return total

    def first(begin, slots):
        return jnp.minimum(begin, n_list - slots)

    load_lists.wait()
    mine = first(before(r, col_base), slots_c)
    load_panel.wait()
    load_inv.start()
    got[r] = panel[pl.ds(mine, slots_c)]
    pl.semaphore_wait(barrier, n_row * n_col - 1)

    cur[slots_c] = jnp.zeros((width, width), cur.dtype)
    tot[slots_r] = jnp.zeros((width, width), tot.dtype)
    chunk = slots_c // CHUNKS

    def go(k, q, step, sems):
        piece = got.at[k, pl.ds(q * chunk, chunk)]
        return pltpu.make_async_remote_copy(
            piece, piece, sems.at[k, q], x_r.at[k, q],
            device_id={"row": r + step}, device_id_type=MESH)

    def go_up(k, q):
        return go(k, q, 1, up_s)

    def go_down(k, q):
        return go(k, q, -1, down_s)

    def send_rows(k):
        return pltpu.make_async_remote_copy(
            got.at[k], quadx.at[k % k_col], qx_s.at[k], qx_r.at[k % k_col],
            device_id={"col": k // k_col}, device_id_type=MESH)

    def send_to_sibling(k, h):
        return pltpu.make_async_remote_copy(
            stage.at[k], sib_in.at[k], st_s.at[k], sib_r.at[k],
            device_id={"col": sibling}, device_id_type=MESH)

    def send_sum(k, target, which):
        return pltpu.make_async_remote_copy(
            x_stage.at[k], dest_x.at[k, chip, core], xs_s.at[k, which], dx_r.at[k, chip, core],
            device_id={"col": target}, device_id_type=MESH)

    def take_sum(k, q, h):
        return pltpu.make_async_remote_copy(
            x_stage.at[k], dest_x.at[k, q, h], xs_s.at[k, 0], dx_r.at[k, q, h],
            device_id={"col": q * 2 + h}, device_id_type=MESH)

    def share(k, target):
        return pltpu.make_async_remote_copy(
            quad_out.at[k], quad_in.at[r, k % k_col], q_s.at[k, target], q_r.at[r, k % k_col],
            device_id={"row": target, "col": k // k_col}, device_id_type=MESH)

    def take_share(at, other):
        return pltpu.make_async_remote_copy(
            quad_out.at[0], quad_in.at[other, at], q_s.at[0, 0], q_r.at[other, at],
            device_id={"row": other}, device_id_type=MESH)

    def crosses(k):
        return (k // k_col) // 2 != c_src // 2

    def lends_rows(k):
        return (c == c_src) & (k // k_col == sibling)

    def has_quad(k):
        return (crosses(k) & (c == c_src)) | (jnp.logical_not(crosses(k)) & (k // k_col == c))

    def pass_on(k, q):
        @pl.when(k != r)
        def _():
            go_up(k, q).wait_recv()

        @pl.when((k <= r) & (r < n_row - 1))
        def _():
            go_up(k, q).start()

        @pl.when((k >= r) & (r > 0))
        def _():
            go_down(k, q).start()

    def use(k):
        owner = k // k_col

        @pl.when(lends_rows(k))
        def _():
            send_rows(k).start()

        begin = before(k, col_base)
        base = first(begin, slots_c)
        cur[0:slots_c] = got[k]
        p = begin
        for j in range(cols_here):
            hit = lists[k, jnp.minimum(p, n_list - 1)] == col_base + j
            slot = jnp.where(hit, jnp.clip(p - base, 0, slots_c - 1), slots_c)
            xs[j * width : (j + 1) * width, :] = cur[slot]
            p += hit.astype(jnp.int32)

        @pl.when(k == r)
        def _():
            load_inv.wait()

        row_first = first(before(k, row_base), slots_r)

        def half_step(turn, carry):
            h = (core + 1 + turn) % 2
            lines = []
            for s in range(half):
                i = jnp.clip(lists[k, row_first + h * half + s] - row_base, 0, rows_here - 1)
                blocks = inv[i]
                lines.append(jnp.concatenate([blocks[j] for j in range(cols_here)], axis=1))
            left = jnp.concatenate(lines, axis=0)
            part[...] = jnp.dot(left, xs[...], preferred_element_type=jnp.float32)

            @pl.when(turn == 0)
            def _():
                stage[k] = part[...].astype(stage.dtype)
                send_to_sibling(k, h).start()

            @pl.when(turn == 1)
            def _():
                send_to_sibling(k, h).wait_recv()
                acc[k] = part[...] + sib_in[k].astype(jnp.float32)
                x_stage[k] = acc[k].astype(x_stage.dtype)

                @pl.when(owner != c)
                def _():
                    send_sum(k, owner, 0).start()

                @pl.when(crosses(k) & (c != c_src))
                def _():
                    send_sum(k, c_src, 1).start()

            return carry

        lax.fori_loop(0, 2, half_step, 0)

    def finish(k):
        owner = k // k_col
        at = k % k_col

        def gather_half(h, carry):
            def from_chip(q, carry):
                @pl.when((q != chip) | (h != core))
                def _():
                    take_sum(k, q, h).wait_recv()
                    come = dest_x[k, q, h].astype(jnp.float32).reshape(half, width, width)
                    where = pl.ds(h * half, half)

                    @pl.when(q == 0)
                    def _():
                        tot[where] = come

                    @pl.when(q > 0)
                    def _():
                        tot[where] = tot[where] + come

                @pl.when((q == chip) & (h == core))
                def _():
                    come = acc[k].reshape(half, width, width)
                    where = pl.ds(h * half, half)

                    @pl.when(q == 0)
                    def _():
                        tot[where] = come

                    @pl.when(q > 0)
                    def _():
                        tot[where] = tot[where] + come

                return carry

            return lax.fori_loop(0, n_chip, from_chip, carry)

        lax.fori_loop(0, 2, gather_half, 0)
        begin = before(k, row_base)
        row_first = first(begin, slots_r)

        @pl.when(has_quad(k))
        def _():
            col_first = first(before(k, c_src * cols_here), slots_c)

            @pl.when(c == c_src)
            def _():
                cur[0:slots_c] = got[k]

            @pl.when(c != c_src)
            def _():
                send_rows(k).wait_recv()
                cur[0:slots_c] = quadx[at]

            lines = []
            for s in range(slots_r):
                position = row_first + s
                number = lists[k, position] - row_base
                valid = (number >= 0) & (number < rows_here)
                slot = jnp.where(valid, jnp.clip(position - col_first, 0, slots_c - 1), slots_c)
                lines.append(cur[slot])
            left = jnp.concatenate(lines, axis=0)
            right = tot[0:slots_r].reshape(slots_r * width, width)
            high = right.astype(jnp.bfloat16)
            low = (right - high.astype(jnp.float32)).astype(jnp.bfloat16)
            both = lax.dot_general(
                left, jnp.concatenate([high, low], axis=1), (((0,), (0,)), ((), ())),
                preferred_element_type=jnp.float32)
            quad_out[k] = (both[:, :width] + both[:, width:]).astype(quad_out.dtype)

            def start_share(other, carry):
                @pl.when((other != r) | (owner != c))
                def _():
                    share(k, other).start()

                return carry

            lax.fori_loop(0, n_row, start_share, 0)

            @pl.when(owner == c)
            def _():
                quad_in[r, at] = quad_out[k]

        @pl.when(owner == c)
        def _():
            p = begin
            for i in range(rows_here):
                hit = lists[k, jnp.minimum(p, n_list - 1)] == row_base + i
                slot = jnp.where(hit, jnp.clip(p - row_first, 0, slots_r - 1), slots_r)
                off[at, i] = (-tot[slot]).astype(off.dtype)
                p += hit.astype(jnp.int32)

    def inside(k):
        return (k >= 0) & (k < n_row)

    def step(s, carry):
        def each(lap, body):
            k = r + jnp.where(lap == 0, -s, s)

            @pl.when(inside(k) & ((s > 0) | (lap == 0)))
            def _():
                body(k)

        def pass_step(i, carry):
            each(i % 2, lambda k: pass_on(k, i // 2))
            return carry

        lax.fori_loop(0, 2 * CHUNKS - 2, pass_step, 0)

        def use_step(lap, carry):
            each(lap, use)
            return carry

        def finish_step(lap, carry):
            last = s - 1
            k = r + jnp.where(lap == 0, -last, last)

            @pl.when(inside(k) & ((last > 0) | ((last == 0) & (lap == 0))))
            def _():
                owner = k // k_col

                @pl.when((owner == c) | (crosses(k) & (c == c_src)))
                def _():
                    finish(k)

            return carry

        lax.fori_loop(0, 2, finish_step, 0)
        lax.fori_loop(2 * CHUNKS - 2, 2 * CHUNKS, pass_step, 0)
        lax.fori_loop(0, 2, use_step, 0)
        return carry

    lax.fori_loop(0, n_row + 1, step, 0)

    def drain(k, carry):
        owner = k // k_col
        for q in range(CHUNKS):
            @pl.when((k <= r) & (r < n_row - 1))
            def _():
                go_up(k, q).wait_send()

            @pl.when((k >= r) & (r > 0))
            def _():
                go_down(k, q).wait_send()

        @pl.when(lends_rows(k))
        def _():
            send_rows(k).wait_send()

        send_to_sibling(k, 0).wait_send()

        @pl.when(owner != c)
        def _():
            send_sum(k, owner, 0).wait_send()

        @pl.when(crosses(k) & (c != c_src))
        def _():
            send_sum(k, c_src, 1).wait_send()

        @pl.when(has_quad(k))
        def _():
            def wait_share(other, carry):
                @pl.when((other != r) | (owner != c))
                def _():
                    share(k, other).wait_send()

                return carry

            lax.fori_loop(0, n_row, wait_share, 0)

        return carry

    lax.fori_loop(0, n_row, drain, 0)

    def arrive(at, carry):
        def one(other, carry):
            k = c * k_col + at

            @pl.when((other != r) | crosses(k))
            def _():
                take_share(at, other).wait_recv()

            return carry

        return lax.fori_loop(0, n_row, one, carry)

    lax.fori_loop(0, k_col, arrive, 0)

    quad = quad_in[0].astype(jnp.float32)
    for other in range(1, n_row):
        quad = quad + quad_in[other].astype(jnp.float32)
    diag[...] = quad


def close(product, quad, dinv, off, diag, update, base, sems):
    keep = pltpu.make_async_copy(product, off, sems.at[0])
    load_update = pltpu.make_async_copy(quad, update, sems.at[1])
    load_base = pltpu.make_async_copy(dinv, base, sems.at[2])
    keep.start()
    load_update.start()
    load_base.start()
    load_update.wait()
    load_base.wait()
    update[...] = base[...] + update[...]
    store = pltpu.make_async_copy(update, diag, sems.at[3])
    store.start()
    keep.wait()
    store.wait()


def per_device(n_row, n_col, inverse_blocks, panel, lists, diag_inverse):
    rows_here, cols_here, width, _ = inverse_blocks.shape
    n_list = panel.shape[1]
    k_col = diag_inverse.shape[0]
    slots_r = slot_count(rows_here, n_list)
    slots_c = slot_count(cols_here, n_list)
    half = slots_r // 2
    n_super = n_row
    low, full = inverse_blocks.dtype, jnp.float32
    part = (half * width, width)
    dma = pltpu.SemaphoreType.DMA
    vmem = pl.BlockSpec(memory_space=pltpu.VMEM)
    hbm = pl.BlockSpec(memory_space=pltpu.HBM)
    anywhere = pl.BlockSpec(memory_space=pl.ANY)
    product, quad = pl.pallas_call(
        functools.partial(
            kernel, n_row, n_col, k_col, rows_here, cols_here, n_list, slots_r, slots_c),
        out_shape=(
            jax.ShapeDtypeStruct((k_col, rows_here, width, width), low),
            jax.ShapeDtypeStruct((k_col, width, width), full),
        ),
        in_specs=[hbm] * 3,
        out_specs=(vmem, vmem),
        scratch_shapes=[
            pltpu.SMEM(lists.shape, lists.dtype),
            pltpu.VMEM(inverse_blocks.shape, low),
            pltpu.VMEM(panel.shape[1:], low),
            pltpu.VMEM((n_super, slots_c, width, width), low),
            pltpu.VMEM((slots_c + 1, width, width), low),
            pltpu.VMEM((cols_here * width, width), low),
            pltpu.VMEM(part, full),
            pltpu.VMEM((n_super,) + part, full),
            pltpu.VMEM((n_super,) + part, low),
            pltpu.VMEM((n_super,) + part, low),
            pltpu.VMEM((n_super,) + part, low),
            pltpu.VMEM((n_super, n_col // 2, 2) + part, low),
            pltpu.VMEM((k_col, slots_c, width, width), low),
            pltpu.VMEM((slots_r + 1, width, width), full),
            pltpu.VMEM((n_super, width, width), low),
            pltpu.VMEM((n_row, k_col, width, width), low),
            dma((3,)),
            dma((n_super, CHUNKS)),
            dma((n_super, CHUNKS)),
            dma((n_super, CHUNKS)),
            dma((n_super,)),
            dma((k_col,)),
            dma((n_super,)),
            dma((n_super,)),
            dma((n_super, 2)),
            dma((n_super, n_col // 2, 2)),
            dma((n_super, n_row)),
            dma((n_row, k_col)),
        ],
        compiler_params=pltpu.CompilerParams(
            collective_id=0, has_side_effects=True, vmem_limit_bytes=53760 * 1024),
        name="selected_inverse",
    )(lists, inverse_blocks, panel)
    return pl.pallas_call(
        close,
        out_shape=(
            jax.ShapeDtypeStruct(product.shape, low),
            jax.ShapeDtypeStruct(quad.shape, full),
        ),
        in_specs=[anywhere] * 3,
        out_specs=(anywhere, anywhere),
        scratch_shapes=[
            pltpu.VMEM(quad.shape, full),
            pltpu.VMEM(quad.shape, full),
            dma((4,)),
        ],
        compiler_params=pltpu.CompilerParams(vmem_limit_bytes=4 * 1024 * 1024),
        name="close",
    )(product, quad, diag_inverse)


def solution(mesh):
    in_specs = (
        P(("pole", "row"), "col", None, None),
        P(("pole", "row"), None, None, None),
        P(),
        P(("pole", "col"), None, None),
    )
    out_specs = (P(("pole", "col"), "row", None, None), P(("pole", "col"), None, None))
    return jax.shard_map(
        functools.partial(per_device, mesh.shape["row"], mesh.shape["col"]),
        mesh=mesh, in_specs=in_specs, out_specs=out_specs, check_vma=False)
```

```python
import functools

import jax
import jax.numpy as jnp
from jax import lax
from jax.experimental import pallas as pl
from jax.experimental.pallas import tpu as pltpu
from jax.sharding import PartitionSpec as P

GROUP = 8
MOST = 6
CHUNKS = 2
MESH = pl.DeviceIdType.MESH


def slot_count(width, n_list):
    if width % GROUP == 0:
        count = width // GROUP * MOST
    elif GROUP % width == 0:
        count = min(width, MOST)
    else:
        count = width
    return min(count, n_list)


def kernel(
    n_row, n_col, k_col, rows_here, cols_here, n_list, slots_r, slots_c, pieces,
    lists_hbm, inv_hbm, panel_hbm, off, diag,
    lists, inv, panel, got, cur, xs, part, acc, stage, x_stage, sib_in, dest_x,
    quadx, tot, quad_out, quad_in,
    load_sem, up_s, down_s, x_r, qx_s, qx_r, st_s, sib_r, xs_s, dx_r, q_s, q_r,
):
    r = lax.axis_index("row")
    c = lax.axis_index("col")
    width = inv.shape[-1]
    chip, core = c // 2, c % 2
    sibling = chip * 2 + 1 - core
    half = slots_r // 2
    piece = half // pieces
    n_chip = n_col // 2
    row_base, col_base = r * rows_here, c * cols_here
    c_src = row_base // cols_here

    load_panel = pltpu.make_async_copy(panel_hbm.at[0], panel, load_sem.at[0])
    load_inv = pltpu.make_async_copy(inv_hbm, inv, load_sem.at[1])
    load_lists = pltpu.make_async_copy(lists_hbm, lists, load_sem.at[2])
    load_lists.start()
    load_panel.start()

    barrier = pltpu.get_barrier_semaphore()
    def greet(at, carry):
        @pl.when((at // n_col != r) | (at % n_col != c))
        def _():
            pl.semaphore_signal(
                barrier, inc=1, device_id={"row": at // n_col, "col": at % n_col}, device_id_type=MESH)

        return carry

    lax.fori_loop(0, n_row * n_col, greet, 0)

    def before(k, bound):
        total = jnp.int32(0)
        for l in range(n_list):
            total += jnp.where(lists[k, l] < bound, 1, 0).astype(jnp.int32)
        return total

    def first(begin, slots):
        return jnp.minimum(begin, n_list - slots)

    load_lists.wait()
    mine = first(before(r, col_base), slots_c)
    load_panel.wait()
    load_inv.start()
    got[r] = panel[pl.ds(mine, slots_c)]
    pl.semaphore_wait(barrier, n_row * n_col - 1)

    cur[slots_c] = jnp.zeros((width, width), cur.dtype)
    tot[slots_r] = jnp.zeros((width, width), tot.dtype)
    chunk = slots_c // CHUNKS

    def go(k, q, step, sems):
        piece = got.at[k, pl.ds(q * chunk, chunk)]
        return pltpu.make_async_remote_copy(
            piece, piece, sems.at[k, q], x_r.at[k, q],
            device_id={"row": r + step}, device_id_type=MESH)

    def go_up(k, q):
        return go(k, q, 1, up_s)

    def go_down(k, q):
        return go(k, q, -1, down_s)

    def send_rows(k):
        return pltpu.make_async_remote_copy(
            got.at[k], quadx.at[k % k_col], qx_s.at[k], qx_r.at[k % k_col],
            device_id={"col": k // k_col}, device_id_type=MESH)

    def send_to_sibling(k, w):
        return pltpu.make_async_remote_copy(
            stage.at[k, w], sib_in.at[k, w], st_s.at[k, w], sib_r.at[k, w],
            device_id={"col": sibling}, device_id_type=MESH)

    def send_sum(k, target, which, w):
        return pltpu.make_async_remote_copy(
            x_stage.at[k, w], dest_x.at[k, chip, core, w], xs_s.at[k, which, w],
            dx_r.at[k, chip, core, w],
            device_id={"col": target}, device_id_type=MESH)

    def take_sum(k, q, h, w):
        return pltpu.make_async_remote_copy(
            x_stage.at[k, w], dest_x.at[k, q, h, w], xs_s.at[k, 0, w], dx_r.at[k, q, h, w],
            device_id={"col": q * 2 + h}, device_id_type=MESH)

    def share(k, target):
        return pltpu.make_async_remote_copy(
            quad_out.at[k], quad_in.at[r, k % k_col], q_s.at[k, target], q_r.at[r, k % k_col],
            device_id={"row": target, "col": k // k_col}, device_id_type=MESH)

    def take_share(at, other):
        return pltpu.make_async_remote_copy(
            quad_out.at[0], quad_in.at[other, at], q_s.at[0, 0], q_r.at[other, at],
            device_id={"row": other}, device_id_type=MESH)

    def crosses(k):
        return (k // k_col) // 2 != c_src // 2

    def lends_rows(k):
        return (c == c_src) & (k // k_col == sibling)

    def has_quad(k):
        return (crosses(k) & (c == c_src)) | (jnp.logical_not(crosses(k)) & (k // k_col == c))

    def pass_on(k, q):
        @pl.when(k != r)
        def _():
            go_up(k, q).wait_recv()

        @pl.when((k <= r) & (r < n_row - 1))
        def _():
            go_up(k, q).start()

        @pl.when((k >= r) & (r > 0))
        def _():
            go_down(k, q).start()

    def use(k):
        owner = k // k_col

        @pl.when(lends_rows(k))
        def _():
            send_rows(k).start()

        begin = before(k, col_base)
        base = first(begin, slots_c)
        cur[0:slots_c] = got[k]
        p = begin
        for j in range(cols_here):
            hit = lists[k, jnp.minimum(p, n_list - 1)] == col_base + j
            slot = jnp.where(hit, jnp.clip(p - base, 0, slots_c - 1), slots_c)
            xs[j * width : (j + 1) * width, :] = cur[slot]
            p += hit.astype(jnp.int32)

        @pl.when(k == r)
        def _():
            load_inv.wait()

        row_first = first(before(k, row_base), slots_r)

        def half_step(turn, carry):
            h = (core + 1 + turn // pieces) % 2
            w = turn % pieces
            lines = []
            for s in range(piece):
                i = jnp.clip(lists[k, row_first + h * half + w * piece + s] - row_base, 0, rows_here - 1)
                blocks = inv[i]
                lines.append(jnp.concatenate([blocks[j] for j in range(cols_here)], axis=1))
            left = jnp.concatenate(lines, axis=0)
            part[...] = jnp.dot(left, xs[...], preferred_element_type=jnp.float32)

            @pl.when(turn < pieces)
            def _():
                stage[k, w] = part[...].astype(stage.dtype)
                send_to_sibling(k, w).start()

            @pl.when(turn >= pieces)
            def _():
                send_to_sibling(k, w).wait_recv()
                acc[k, w] = part[...] + sib_in[k, w].astype(jnp.float32)
                x_stage[k, w] = acc[k, w].astype(x_stage.dtype)

                @pl.when(owner != c)
                def _():
                    send_sum(k, owner, 0, w).start()

                @pl.when(crosses(k) & (c != c_src))
                def _():
                    send_sum(k, c_src, 1, w).start()

            return carry

        lax.fori_loop(0, 2 * pieces, half_step, 0)

    def finish(k):
        owner = k // k_col
        at = k % k_col

        def gather_piece(part_at, carry):
            h, w = part_at % 2, part_at // 2

            def from_chip(q, carry):
                @pl.when((q != chip) | (h != core))
                def _():
                    take_sum(k, q, h, w).wait_recv()
                    come = dest_x[k, q, h, w].astype(jnp.float32).reshape(piece, width, width)
                    where = pl.ds(h * half + w * piece, piece)

                    @pl.when(q == 0)
                    def _():
                        tot[where] = come

                    @pl.when(q > 0)
                    def _():
                        tot[where] = tot[where] + come

                @pl.when((q == chip) & (h == core))
                def _():
                    come = acc[k, w].reshape(piece, width, width)
                    where = pl.ds(h * half + w * piece, piece)

                    @pl.when(q == 0)
                    def _():
                        tot[where] = come

                    @pl.when(q > 0)
                    def _():
                        tot[where] = tot[where] + come

                return carry

            return lax.fori_loop(0, n_chip, from_chip, carry)

        lax.fori_loop(0, 2 * pieces, gather_piece, 0)
        begin = before(k, row_base)
        row_first = first(begin, slots_r)

        @pl.when(has_quad(k))
        def _():
            col_first = first(before(k, c_src * cols_here), slots_c)

            @pl.when(c == c_src)
            def _():
                cur[0:slots_c] = got[k]

            @pl.when(c != c_src)
            def _():
                send_rows(k).wait_recv()
                cur[0:slots_c] = quadx[at]

            lines = []
            for s in range(slots_r):
                position = row_first + s
                number = lists[k, position] - row_base
                valid = (number >= 0) & (number < rows_here)
                slot = jnp.where(valid, jnp.clip(position - col_first, 0, slots_c - 1), slots_c)
                lines.append(cur[slot])
            left = jnp.concatenate(lines, axis=0)
            right = tot[0:slots_r].reshape(slots_r * width, width)
            high = right.astype(jnp.bfloat16)
            low = (right - high.astype(jnp.float32)).astype(jnp.bfloat16)
            both = lax.dot_general(
                left, jnp.concatenate([high, low], axis=1), (((0,), (0,)), ((), ())),
                preferred_element_type=jnp.float32)
            quad_out[k] = (both[:, :width] + both[:, width:]).astype(quad_out.dtype)

            def start_share(other, carry):
                @pl.when((other != r) | (owner != c))
                def _():
                    share(k, other).start()

                return carry

            lax.fori_loop(0, n_row, start_share, 0)

            @pl.when(owner == c)
            def _():
                quad_in[r, at] = quad_out[k]

        @pl.when(owner == c)
        def _():
            p = begin
            for i in range(rows_here):
                hit = lists[k, jnp.minimum(p, n_list - 1)] == row_base + i
                slot = jnp.where(hit, jnp.clip(p - row_first, 0, slots_r - 1), slots_r)
                off[at, i] = (-tot[slot]).astype(off.dtype)
                p += hit.astype(jnp.int32)

    def inside(k):
        return (k >= 0) & (k < n_row)

    def step(s, carry):
        def each(lap, body):
            k = r + jnp.where(lap == 0, -s, s)

            @pl.when(inside(k) & ((s > 0) | (lap == 0)))
            def _():
                body(k)

        def pass_step(i, carry):
            each(i % 2, lambda k: pass_on(k, i // 2))
            return carry

        lax.fori_loop(0, 2 * CHUNKS - 2, pass_step, 0)

        def use_step(lap, carry):
            each(lap, use)
            return carry

        def finish_step(lap, carry):
            last = s - 1
            k = r + jnp.where(lap == 0, -last, last)

            @pl.when(inside(k) & ((last > 0) | ((last == 0) & (lap == 0))))
            def _():
                owner = k // k_col

                @pl.when((owner == c) | (crosses(k) & (c == c_src)))
                def _():
                    finish(k)

            return carry

        lax.fori_loop(0, 2, finish_step, 0)
        lax.fori_loop(2 * CHUNKS - 2, 2 * CHUNKS, pass_step, 0)
        lax.fori_loop(0, 2, use_step, 0)
        return carry

    lax.fori_loop(0, n_row + 1, step, 0)

    def drain(k, carry):
        owner = k // k_col
        for q in range(CHUNKS):
            @pl.when((k <= r) & (r < n_row - 1))
            def _():
                go_up(k, q).wait_send()

            @pl.when((k >= r) & (r > 0))
            def _():
                go_down(k, q).wait_send()

        @pl.when(lends_rows(k))
        def _():
            send_rows(k).wait_send()

        for w in range(pieces):
            send_to_sibling(k, w).wait_send()

            @pl.when(owner != c)
            def _():
                send_sum(k, owner, 0, w).wait_send()

            @pl.when(crosses(k) & (c != c_src))
            def _():
                send_sum(k, c_src, 1, w).wait_send()

        @pl.when(has_quad(k))
        def _():
            def wait_share(other, carry):
                @pl.when((other != r) | (owner != c))
                def _():
                    share(k, other).wait_send()

                return carry

            lax.fori_loop(0, n_row, wait_share, 0)

        return carry

    lax.fori_loop(0, n_row, drain, 0)

    def arrive(at, carry):
        def one(other, carry):
            k = c * k_col + at

            @pl.when((other != r) | crosses(k))
            def _():
                take_share(at, other).wait_recv()

            return carry

        return lax.fori_loop(0, n_row, one, carry)

    lax.fori_loop(0, k_col, arrive, 0)

    quad = quad_in[0].astype(jnp.float32)
    for other in range(1, n_row):
        quad = quad + quad_in[other].astype(jnp.float32)
    diag[...] = quad


def close(product, quad, dinv, off, diag, update, base, sems):
    keep = pltpu.make_async_copy(product, off, sems.at[0])
    load_update = pltpu.make_async_copy(quad, update, sems.at[1])
    load_base = pltpu.make_async_copy(dinv, base, sems.at[2])
    keep.start()
    load_update.start()
    load_base.start()
    load_update.wait()
    load_base.wait()
    update[...] = base[...] + update[...]
    store = pltpu.make_async_copy(update, diag, sems.at[3])
    store.start()
    keep.wait()
    store.wait()


def per_device(n_row, n_col, inverse_blocks, panel, lists, diag_inverse):
    rows_here, cols_here, width, _ = inverse_blocks.shape
    n_list = panel.shape[1]
    k_col = diag_inverse.shape[0]
    slots_r = slot_count(rows_here, n_list)
    slots_c = slot_count(cols_here, n_list)
    half = slots_r // 2
    n_super = n_row
    low, full = inverse_blocks.dtype, jnp.float32
    pieces = 2 if half % 2 == 0 else 1
    part = (half // pieces * width, width)
    dma = pltpu.SemaphoreType.DMA
    vmem = pl.BlockSpec(memory_space=pltpu.VMEM)
    hbm = pl.BlockSpec(memory_space=pltpu.HBM)
    anywhere = pl.BlockSpec(memory_space=pl.ANY)
    product, quad = pl.pallas_call(
        functools.partial(
            kernel, n_row, n_col, k_col, rows_here, cols_here, n_list, slots_r, slots_c, pieces),
        out_shape=(
            jax.ShapeDtypeStruct((k_col, rows_here, width, width), low),
            jax.ShapeDtypeStruct((k_col, width, width), full),
        ),
        in_specs=[hbm] * 3,
        out_specs=(vmem, vmem),
        scratch_shapes=[
            pltpu.SMEM(lists.shape, lists.dtype),
            pltpu.VMEM(inverse_blocks.shape, low),
            pltpu.VMEM(panel.shape[1:], low),
            pltpu.VMEM((n_super, slots_c, width, width), low),
            pltpu.VMEM((slots_c + 1, width, width), low),
            pltpu.VMEM((cols_here * width, width), low),
            pltpu.VMEM(part, full),
            pltpu.VMEM((n_super, pieces) + part, full),
            pltpu.VMEM((n_super, pieces) + part, low),
            pltpu.VMEM((n_super, pieces) + part, low),
            pltpu.VMEM((n_super, pieces) + part, low),
            pltpu.VMEM((n_super, n_col // 2, 2, pieces) + part, low),
            pltpu.VMEM((k_col, slots_c, width, width), low),
            pltpu.VMEM((slots_r + 1, width, width), full),
            pltpu.VMEM((n_super, width, width), low),
            pltpu.VMEM((n_row, k_col, width, width), low),
            dma((3,)),
            dma((n_super, CHUNKS)),
            dma((n_super, CHUNKS)),
            dma((n_super, CHUNKS)),
            dma((n_super,)),
            dma((k_col,)),
            dma((n_super, pieces)),
            dma((n_super, pieces)),
            dma((n_super, 2, pieces)),
            dma((n_super, n_col // 2, 2, pieces)),
            dma((n_super, n_row)),
            dma((n_row, k_col)),
        ],
        compiler_params=pltpu.CompilerParams(
            collective_id=0, has_side_effects=True, vmem_limit_bytes=53760 * 1024),
        name="selected_inverse",
    )(lists, inverse_blocks, panel)
    return pl.pallas_call(
        close,
        out_shape=(
            jax.ShapeDtypeStruct(product.shape, low),
            jax.ShapeDtypeStruct(quad.shape, full),
        ),
        in_specs=[anywhere] * 3,
        out_specs=(anywhere, anywhere),
        scratch_shapes=[
            pltpu.VMEM(quad.shape, full),
            pltpu.VMEM(quad.shape, full),
            dma((4,)),
        ],
        compiler_params=pltpu.CompilerParams(vmem_limit_bytes=4 * 1024 * 1024),
        name="close",
    )(product, quad, diag_inverse)


def solution(mesh):
    in_specs = (
        P(("pole", "row"), "col", None, None),
        P(("pole", "row"), None, None, None),
        P(),
        P(("pole", "col"), None, None),
    )
    out_specs = (P(("pole", "col"), "row", None, None), P(("pole", "col"), None, None))
    return jax.shard_map(
        functools.partial(per_device, mesh.shape["row"], mesh.shape["col"]),
        mesh=mesh, in_specs=in_specs, out_specs=out_specs, check_vma=False)
```

```python
import functools

import jax
import jax.numpy as jnp
from jax import lax
from jax.experimental import pallas as pl
from jax.experimental.pallas import tpu as pltpu
from jax.sharding import PartitionSpec as P

GROUP = 8
MOST = 6
CHUNKS = 2
MESH = pl.DeviceIdType.MESH


def slot_count(width, n_list):
    if width % GROUP == 0:
        count = width // GROUP * MOST
    elif GROUP % width == 0:
        count = min(width, MOST)
    else:
        count = width
    return min(count, n_list)


def kernel(
    n_row, n_col, k_col, rows_here, cols_here, n_list, slots_r, slots_c, pieces,
    lists_hbm, inv_hbm, panel_hbm, off, diag,
    lists, inv, panel, got, cur, xs, part, acc, stage, x_stage, sib_in, dest_x,
    quadx, tot, quad_out, quad_in,
    load_sem, up_s, down_s, x_r, qx_s, qx_r, st_s, sib_r, xs_s, dx_r, q_s, q_r,
):
    r = lax.axis_index("row")
    c = lax.axis_index("col")
    width = inv.shape[-1]
    chip, core = c // 2, c % 2
    sibling = chip * 2 + 1 - core
    half = slots_r // 2
    piece = half // pieces
    n_chip = n_col // 2
    row_base, col_base = r * rows_here, c * cols_here
    c_src = row_base // cols_here

    load_panel = pltpu.make_async_copy(panel_hbm.at[0], panel, load_sem.at[0])
    load_inv = pltpu.make_async_copy(inv_hbm, inv, load_sem.at[1])
    load_lists = pltpu.make_async_copy(lists_hbm, lists, load_sem.at[2])
    load_lists.start()
    load_panel.start()

    barrier = pltpu.get_barrier_semaphore()
    def greet(at, carry):
        @pl.when((at // n_col != r) | (at % n_col != c))
        def _():
            pl.semaphore_signal(
                barrier, inc=1, device_id={"row": at // n_col, "col": at % n_col}, device_id_type=MESH)

        return carry

    lax.fori_loop(0, n_row * n_col, greet, 0)

    def before(k, bound):
        total = jnp.int32(0)
        for l in range(n_list):
            total += jnp.where(lists[k, l] < bound, 1, 0).astype(jnp.int32)
        return total

    def first(begin, slots):
        return jnp.minimum(begin, n_list - slots)

    load_lists.wait()
    mine = first(before(r, col_base), slots_c)
    load_panel.wait()
    load_inv.start()
    got[r] = panel[pl.ds(mine, slots_c)]
    pl.semaphore_wait(barrier, n_row * n_col - 1)

    cur[slots_c] = jnp.zeros((width, width), cur.dtype)
    tot[slots_r] = jnp.zeros((width, width), tot.dtype)
    chunk = slots_c // CHUNKS

    def go(k, q, step, sems):
        piece = got.at[k, pl.ds(q * chunk, chunk)]
        return pltpu.make_async_remote_copy(
            piece, piece, sems.at[k, q], x_r.at[k, q],
            device_id={"row": r + step}, device_id_type=MESH)

    def go_up(k, q):
        return go(k, q, 1, up_s)

    def go_down(k, q):
        return go(k, q, -1, down_s)

    def send_rows(k):
        return pltpu.make_async_remote_copy(
            got.at[k], quadx.at[k % k_col], qx_s.at[k], qx_r.at[k % k_col],
            device_id={"col": k // k_col}, device_id_type=MESH)

    def send_to_sibling(k, w):
        return pltpu.make_async_remote_copy(
            stage.at[k, w], sib_in.at[k, w], st_s.at[k, w], sib_r.at[k, w],
            device_id={"col": sibling}, device_id_type=MESH)

    def send_sum(k, target, which, w):
        return pltpu.make_async_remote_copy(
            x_stage.at[k, w], dest_x.at[k, chip, core, w], xs_s.at[k, which, w],
            dx_r.at[k, chip, core, w],
            device_id={"col": target}, device_id_type=MESH)

    def take_sum(k, q, h, w):
        return pltpu.make_async_remote_copy(
            x_stage.at[k, w], dest_x.at[k, q, h, w], xs_s.at[k, 0, w], dx_r.at[k, q, h, w],
            device_id={"col": q * 2 + h}, device_id_type=MESH)

    def share(k, target):
        return pltpu.make_async_remote_copy(
            quad_out.at[k], quad_in.at[r, k % k_col], q_s.at[k, target], q_r.at[r, k % k_col],
            device_id={"row": target, "col": k // k_col}, device_id_type=MESH)

    def take_share(at, other):
        return pltpu.make_async_remote_copy(
            quad_out.at[0], quad_in.at[other, at], q_s.at[0, 0], q_r.at[other, at],
            device_id={"row": other}, device_id_type=MESH)

    def crosses(k):
        return (k // k_col) // 2 != c_src // 2

    def lends_rows(k):
        return (c == c_src) & (k // k_col == sibling)

    def has_quad(k):
        return (crosses(k) & (c == c_src)) | (jnp.logical_not(crosses(k)) & (k // k_col == c))

    def pass_on(k, q):
        @pl.when(k != r)
        def _():
            go_up(k, q).wait_recv()

        @pl.when((k <= r) & (r < n_row - 1))
        def _():
            go_up(k, q).start()

        @pl.when((k >= r) & (r > 0))
        def _():
            go_down(k, q).start()

    def use(k):
        owner = k // k_col

        @pl.when(lends_rows(k))
        def _():
            send_rows(k).start()

        begin = before(k, col_base)
        base = first(begin, slots_c)
        cur[0:slots_c] = got[k]
        columns = []
        for t in range(slots_c):
            number = lists[k, base + t] - col_base
            valid = (number >= 0) & (number < cols_here)
            xs[t * width : (t + 1) * width, :] = cur[jnp.where(valid, t, slots_c)]
            columns.append(jnp.clip(number, 0, cols_here - 1))

        @pl.when(k == r)
        def _():
            load_inv.wait()

        row_first = first(before(k, row_base), slots_r)

        def half_step(turn, carry):
            h = (core + 1 + turn // pieces) % 2
            w = turn % pieces
            lines = []
            for s in range(piece):
                i = jnp.clip(lists[k, row_first + h * half + w * piece + s] - row_base, 0, rows_here - 1)
                lines.append(jnp.concatenate([inv[i, j] for j in columns], axis=1))
            left = jnp.concatenate(lines, axis=0)
            part[...] = jnp.dot(left, xs[...], preferred_element_type=jnp.float32)

            @pl.when(turn < pieces)
            def _():
                stage[k, w] = part[...].astype(stage.dtype)
                send_to_sibling(k, w).start()

            @pl.when(turn >= pieces)
            def _():
                send_to_sibling(k, w).wait_recv()
                acc[k, w] = part[...] + sib_in[k, w].astype(jnp.float32)
                x_stage[k, w] = acc[k, w].astype(x_stage.dtype)

                @pl.when(owner != c)
                def _():
                    send_sum(k, owner, 0, w).start()

                @pl.when(crosses(k) & (c != c_src))
                def _():
                    send_sum(k, c_src, 1, w).start()

            return carry

        lax.fori_loop(0, 2 * pieces, half_step, 0)

    def finish(k):
        owner = k // k_col
        at = k % k_col

        def gather_piece(part_at, carry):
            h, w = part_at % 2, part_at // 2

            def from_chip(q, carry):
                @pl.when((q != chip) | (h != core))
                def _():
                    take_sum(k, q, h, w).wait_recv()
                    come = dest_x[k, q, h, w].astype(jnp.float32).reshape(piece, width, width)
                    where = pl.ds(h * half + w * piece, piece)

                    @pl.when(q == 0)
                    def _():
                        tot[where] = come

                    @pl.when(q > 0)
                    def _():
                        tot[where] = tot[where] + come

                @pl.when((q == chip) & (h == core))
                def _():
                    come = acc[k, w].reshape(piece, width, width)
                    where = pl.ds(h * half + w * piece, piece)

                    @pl.when(q == 0)
                    def _():
                        tot[where] = come

                    @pl.when(q > 0)
                    def _():
                        tot[where] = tot[where] + come

                return carry

            return lax.fori_loop(0, n_chip, from_chip, carry)

        lax.fori_loop(0, 2 * pieces, gather_piece, 0)
        begin = before(k, row_base)
        row_first = first(begin, slots_r)

        @pl.when(has_quad(k))
        def _():
            col_first = first(before(k, c_src * cols_here), slots_c)

            @pl.when(c == c_src)
            def _():
                cur[0:slots_c] = got[k]

            @pl.when(c != c_src)
            def _():
                send_rows(k).wait_recv()
                cur[0:slots_c] = quadx[at]

            lines = []
            for s in range(slots_r):
                position = row_first + s
                number = lists[k, position] - row_base
                valid = (number >= 0) & (number < rows_here)
                slot = jnp.where(valid, jnp.clip(position - col_first, 0, slots_c - 1), slots_c)
                lines.append(cur[slot])
            left = jnp.concatenate(lines, axis=0)
            right = tot[0:slots_r].reshape(slots_r * width, width)
            high = right.astype(jnp.bfloat16)
            low = (right - high.astype(jnp.float32)).astype(jnp.bfloat16)
            both = lax.dot_general(
                left, jnp.concatenate([high, low], axis=1), (((0,), (0,)), ((), ())),
                preferred_element_type=jnp.float32)
            quad_out[k] = (both[:, :width] + both[:, width:]).astype(quad_out.dtype)

            def start_share(other, carry):
                @pl.when((other != r) | (owner != c))
                def _():
                    share(k, other).start()

                return carry

            lax.fori_loop(0, n_row, start_share, 0)

            @pl.when(owner == c)
            def _():
                quad_in[r, at] = quad_out[k]

        @pl.when(owner == c)
        def _():
            p = begin
            for i in range(rows_here):
                hit = lists[k, jnp.minimum(p, n_list - 1)] == row_base + i
                slot = jnp.where(hit, jnp.clip(p - row_first, 0, slots_r - 1), slots_r)
                off[at, i] = (-tot[slot]).astype(off.dtype)
                p += hit.astype(jnp.int32)

    def inside(k):
        return (k >= 0) & (k < n_row)

    def step(s, carry):
        def each(lap, body):
            k = r + jnp.where(lap == 0, -s, s)

            @pl.when(inside(k) & ((s > 0) | (lap == 0)))
            def _():
                body(k)

        def pass_step(i, carry):
            each(i % 2, lambda k: pass_on(k, i // 2))
            return carry

        lax.fori_loop(0, 2 * CHUNKS - 2, pass_step, 0)

        def use_step(lap, carry):
            each(lap, use)
            return carry

        def finish_step(lap, carry):
            last = s - 1
            k = r + jnp.where(lap == 0, -last, last)

            @pl.when(inside(k) & ((last > 0) | ((last == 0) & (lap == 0))))
            def _():
                owner = k // k_col

                @pl.when((owner == c) | (crosses(k) & (c == c_src)))
                def _():
                    finish(k)

            return carry

        lax.fori_loop(0, 2, finish_step, 0)
        lax.fori_loop(2 * CHUNKS - 2, 2 * CHUNKS, pass_step, 0)
        lax.fori_loop(0, 2, use_step, 0)
        return carry

    lax.fori_loop(0, n_row + 1, step, 0)

    def drain(k, carry):
        owner = k // k_col
        for q in range(CHUNKS):
            @pl.when((k <= r) & (r < n_row - 1))
            def _():
                go_up(k, q).wait_send()

            @pl.when((k >= r) & (r > 0))
            def _():
                go_down(k, q).wait_send()

        @pl.when(lends_rows(k))
        def _():
            send_rows(k).wait_send()

        for w in range(pieces):
            send_to_sibling(k, w).wait_send()

            @pl.when(owner != c)
            def _():
                send_sum(k, owner, 0, w).wait_send()

            @pl.when(crosses(k) & (c != c_src))
            def _():
                send_sum(k, c_src, 1, w).wait_send()

        @pl.when(has_quad(k))
        def _():
            def wait_share(other, carry):
                @pl.when((other != r) | (owner != c))
                def _():
                    share(k, other).wait_send()

                return carry

            lax.fori_loop(0, n_row, wait_share, 0)

        return carry

    lax.fori_loop(0, n_row, drain, 0)

    def arrive(at, carry):
        def one(other, carry):
            k = c * k_col + at

            @pl.when((other != r) | crosses(k))
            def _():
                take_share(at, other).wait_recv()

            return carry

        return lax.fori_loop(0, n_row, one, carry)

    lax.fori_loop(0, k_col, arrive, 0)

    quad = quad_in[0].astype(jnp.float32)
    for other in range(1, n_row):
        quad = quad + quad_in[other].astype(jnp.float32)
    diag[...] = quad


def close(product, quad, dinv, off, diag, update, base, sems):
    keep = pltpu.make_async_copy(product, off, sems.at[0])
    load_update = pltpu.make_async_copy(quad, update, sems.at[1])
    load_base = pltpu.make_async_copy(dinv, base, sems.at[2])
    keep.start()
    load_update.start()
    load_base.start()
    load_update.wait()
    load_base.wait()
    update[...] = base[...] + update[...]
    store = pltpu.make_async_copy(update, diag, sems.at[3])
    store.start()
    keep.wait()
    store.wait()


def per_device(n_row, n_col, inverse_blocks, panel, lists, diag_inverse):
    rows_here, cols_here, width, _ = inverse_blocks.shape
    n_list = panel.shape[1]
    k_col = diag_inverse.shape[0]
    slots_r = slot_count(rows_here, n_list)
    slots_c = slot_count(cols_here, n_list)
    half = slots_r // 2
    n_super = n_row
    low, full = inverse_blocks.dtype, jnp.float32
    pieces = 2 if half % 2 == 0 else 1
    part = (half // pieces * width, width)
    dma = pltpu.SemaphoreType.DMA
    vmem = pl.BlockSpec(memory_space=pltpu.VMEM)
    hbm = pl.BlockSpec(memory_space=pltpu.HBM)
    anywhere = pl.BlockSpec(memory_space=pl.ANY)
    product, quad = pl.pallas_call(
        functools.partial(
            kernel, n_row, n_col, k_col, rows_here, cols_here, n_list, slots_r, slots_c, pieces),
        out_shape=(
            jax.ShapeDtypeStruct((k_col, rows_here, width, width), low),
            jax.ShapeDtypeStruct((k_col, width, width), full),
        ),
        in_specs=[hbm] * 3,
        out_specs=(vmem, vmem),
        scratch_shapes=[
            pltpu.SMEM(lists.shape, lists.dtype),
            pltpu.VMEM(inverse_blocks.shape, low),
            pltpu.VMEM(panel.shape[1:], low),
            pltpu.VMEM((n_super, slots_c, width, width), low),
            pltpu.VMEM((slots_c + 1, width, width), low),
            pltpu.VMEM((slots_c * width, width), low),
            pltpu.VMEM(part, full),
            pltpu.VMEM((n_super, pieces) + part, full),
            pltpu.VMEM((n_super, pieces) + part, low),
            pltpu.VMEM((n_super, pieces) + part, low),
            pltpu.VMEM((n_super, pieces) + part, low),
            pltpu.VMEM((n_super, n_col // 2, 2, pieces) + part, low),
            pltpu.VMEM((k_col, slots_c, width, width), low),
            pltpu.VMEM((slots_r + 1, width, width), full),
            pltpu.VMEM((n_super, width, width), low),
            pltpu.VMEM((n_row, k_col, width, width), low),
            dma((3,)),
            dma((n_super, CHUNKS)),
            dma((n_super, CHUNKS)),
            dma((n_super, CHUNKS)),
            dma((n_super,)),
            dma((k_col,)),
            dma((n_super, pieces)),
            dma((n_super, pieces)),
            dma((n_super, 2, pieces)),
            dma((n_super, n_col // 2, 2, pieces)),
            dma((n_super, n_row)),
            dma((n_row, k_col)),
        ],
        compiler_params=pltpu.CompilerParams(
            collective_id=0, has_side_effects=True, vmem_limit_bytes=53760 * 1024),
        name="selected_inverse",
    )(lists, inverse_blocks, panel)
    return pl.pallas_call(
        close,
        out_shape=(
            jax.ShapeDtypeStruct(product.shape, low),
            jax.ShapeDtypeStruct(quad.shape, full),
        ),
        in_specs=[anywhere] * 3,
        out_specs=(anywhere, anywhere),
        scratch_shapes=[
            pltpu.VMEM(quad.shape, full),
            pltpu.VMEM(quad.shape, full),
            dma((4,)),
        ],
        compiler_params=pltpu.CompilerParams(vmem_limit_bytes=4 * 1024 * 1024),
        name="close",
    )(product, quad, diag_inverse)


def solution(mesh):
    in_specs = (
        P(("pole", "row"), "col", None, None),
        P(("pole", "row"), None, None, None),
        P(),
        P(("pole", "col"), None, None),
    )
    out_specs = (P(("pole", "col"), "row", None, None), P(("pole", "col"), None, None))
    return jax.shard_map(
        functools.partial(per_device, mesh.shape["row"], mesh.shape["col"]),
        mesh=mesh, in_specs=in_specs, out_specs=out_specs, check_vma=False)
```
